128 devices in a mesh: gr: 8 (over x, core), gc: 8 (over y, z_lo), dr: 2 (over z_hi).
Axes of the slice: x: 4, y: 4, z: 4 (z_hi: 2, z_lo: 2; z = z_hi * 2 + z_lo), core: 2. Of those that a mesh axis runs over, the one named last changes fastest.
Arguments:
- draft_rows: bfloat16 [512, 14848], P('gr', ('gc', 'dr')), may hold values from -6 to 6
- tree_sizes: int32 [64], replicated, may hold values from 1 to 128, 512 in all
- draft_map: int32 [64], replicated, may hold values from 0 to 15
- row_order: int32 [512], replicated, may hold values from 0 to 511, each once
- up_weight: bfloat16 [14848, 53248], P(('gc', 'dr'), 'gr'), may hold values from -0.046875 to 0.046875
- down_weight: bfloat16 [53248, 14848], P('gr', ('gc', 'dr')), may hold values from -0.02734375 to 0.02734375
Outputs:
- verified: bfloat16 [512, 14848], P('gr', ('gc', 'dr'))
The draws below stay inside these ranges and needn't reach their ends.
Inputs may be any that keep to these rules, and one draw needn't show every extreme that they name: `tree_sizes`: tree sizes sum to 512; some request has exactly 128. `row_order`: each position appears once.
All inputs are finite; a program needn't handle non-finite values.
Results may differ from the reference program's by a relative error of at most 0.005.
Values may be sent and summed in bfloat16 or wider, within the bound.
No kernel may reach another device: no remote copies, remote signals or barrier semaphores. Data moves between devices by JAX's collectives and lax.ppermute only.
A program may use at most 128 MiB of HBM per device.

```python
import math
import jax
import jax.numpy as jnp
import numpy as np

D = 14848
FF = 53248
ROWS = 512
NDRAFT = 16
REQS = 64
MOST = 128


def set_ends(values, key, least, high):
    shape = values.shape
    place = [jax.random.randint(jax.random.fold_in(key, axis), (), 0, shape[axis]) for axis in range(len(shape))]
    values = values.at[tuple(place)].set(least)
    longest = shape.index(max(shape))
    place[longest] = (place[longest] + 1) % shape[longest]
    return values.at[tuple(place)].set(high)


def block_scale(rng, shape, cuts, low, largest):
    def one(axis_at, blocks):
        heights = jax.random.uniform(jax.random.fold_in(jax.random.fold_in(rng, 6), axis_at), (blocks,), jnp.float32, low / len(cuts), largest / len(cuts))
        return jnp.repeat(jnp.exp(heights), shape[axis_at] // blocks).reshape((-1,) + (1,) * (len(shape) - axis_at - 1))

    factor_of = one(*cuts[0])
    for cut in cuts[1:]:
        factor_of = factor_of * one(*cut)
    return factor_of


def split_up(amount, total, reach, slope):
    loads = [(1 << 20) // math.isqrt(grade ** slope) + 1 for grade in range(2, amount + 1)]
    surplus, given = total - reach - (amount - 1), [1] * (amount - 1)
    while surplus > 0:
        free = [i for i in range(amount - 1) if given[i] < reach]
        pool, left = sum([loads[i] for i in free]), surplus
        for i in free:
            extra = min(reach - given[i], max(1, left * loads[i] // pool), surplus)
            given[i] = given[i] + extra
            surplus = surplus - extra
    return np.array([reach] + given)


def ragged(rng, amount, total, most, skew):
    if amount == 2:
        one = jax.random.randint(rng, (), max(1, total - most), min(most, total - 1) + 1)
        return jnp.stack([one, total - one])
    sizes = jnp.asarray(split_up(amount, total, most, skew), jnp.int32)
    twos = (amount - 1) // 2
    giver, sink = sizes[1:1 + 2 * twos:2], sizes[2:2 + 2 * twos:2]
    room = jnp.minimum(giver - 1, most - sink)
    passed = jax.random.randint(jax.random.fold_in(rng, 1), (twos,), 0, 1 << 20) % (room + 1)
    sizes = sizes.at[1:1 + 2 * twos:2].set(giver - passed).at[2:2 + 2 * twos:2].set(sink + passed)
    return sizes[jax.random.permutation(jax.random.fold_in(rng, 2), amount)]


def scatter_about(rng, shape, deviation, bound, split=(), kind=jnp.bfloat16):
    loudness = block_scale(rng, shape, split, -0.22, 0.18) if split else 1.0
    entries = jax.random.normal(rng, shape, jnp.float32) * deviation * loudness
    return jnp.minimum(jnp.maximum(entries, -bound), bound).astype(kind)


def setup_inputs(seed: int = 0) -> dict:
    streams_of = jax.random.split(jax.random.key(seed), 7)
    draft_rows = scatter_about(streams_of[0], (ROWS, D), 1.0, 6.0, ((0, 8), (1, 16)))
    tree_sizes = ragged(streams_of[1], REQS, ROWS, MOST, 2).astype(jnp.int32)
    draft_map = set_ends(jax.random.randint(streams_of[2], (REQS,), 0, NDRAFT), jax.random.fold_in(streams_of[2], 1), 0, NDRAFT - 1).astype(jnp.int32)
    row_order = jax.random.permutation(streams_of[3], ROWS).astype(jnp.int32)
    up_weight = scatter_about(streams_of[4], (D, FF), D ** -0.5, 0.046875, ((0, 16), (1, 8)))
    down_weight = scatter_about(streams_of[5], (FF, D), FF ** -0.5, 0.02734375, ((0, 8), (1, 16)))
    return dict(draft_rows=draft_rows, tree_sizes=tree_sizes, draft_map=draft_map, row_order=row_order, up_weight=up_weight, down_weight=down_weight)


def source_rows(tree_sizes, draft_map, row_order):
    ends = jnp.cumsum(tree_sizes).astype(jnp.int32)
    req_start = (ends - tree_sizes).astype(jnp.int32)
    reqs = jnp.arange(tree_sizes.shape[0], dtype=jnp.int32)
    before = (draft_map[None, :] < draft_map[:, None]) | ((draft_map[None, :] == draft_map[:, None]) & (reqs[None, :] < reqs[:, None]))
    draft_start = jnp.sum(jnp.where(before, tree_sizes[None, :], 0), axis=1).astype(jnp.int32)
    position = row_order.astype(jnp.int32)
    owner = jnp.sum((position[:, None] >= ends[None, :]).astype(jnp.int32), axis=1).astype(jnp.int32)
    return (draft_start[owner] + position - req_start[owner]).astype(jnp.int32)


def reference(draft_rows, tree_sizes, draft_map, row_order, up_weight, down_weight):
    source = source_rows(tree_sizes, draft_map, row_order)
    candidates = draft_rows[source]
    pre = jnp.dot(candidates, up_weight, preferred_element_type=jnp.float32)
    hidden = jax.nn.gelu(pre, approximate=False).astype(jnp.bfloat16)
    return jnp.dot(hidden, down_weight, preferred_element_type=jnp.float32).astype(jnp.bfloat16)
```

```python
import jax
import jax.numpy as jnp
from jax import lax
from jax.sharding import PartitionSpec as P

BF, F32 = jnp.bfloat16, jnp.float32
YZ = ("gc", "dr")
RS_STEPS = 2


def place(y, z):
    return (y * 2 + z % 2) * 2 + z // 2


SIDES = ((1, 0, 3, 2), (3, 2, 1, 0))
SWAPS = tuple(
    [(place(y, z), place(side[y], z)) for y in range(4) for z in range(4)] for side in SIDES
) + tuple(
    [(place(y, z), place(y, side[z])) for y in range(4) for z in range(4)] for side in SIDES
)


def swap(value, side):
    return lax.ppermute(value, YZ, SWAPS[side])


def from_chip(value, ahead):
    pairs = [(((x + ahead) % 4) * 2 + c, x * 2 + c) for x in range(4) for c in range(2)]
    return lax.ppermute(value, "gr", pairs)


def other_core(value):
    return lax.ppermute(value, "gr", [(i, i ^ 1) for i in range(8)])


def square_bits(p):
    return (p & 1) ^ (p >> 1), p >> 1


def source_rows(tree_sizes, draft_map, order):
    reqs = jnp.arange(tree_sizes.shape[0], dtype=jnp.int32)
    earlier = reqs[None, :] < reqs[:, None]
    req_start = jnp.sum(jnp.where(earlier, tree_sizes[None, :], 0), axis=1)
    before = (draft_map[None, :] < draft_map[:, None]) | (
        draft_map[None, :] == draft_map[:, None]
    ) & earlier
    draft_start = jnp.sum(jnp.where(before, tree_sizes[None, :], 0), axis=1)
    shift = draft_start - req_start
    position = order[:, None]
    inside = (position >= req_start[None, :]) & (position < (req_start + tree_sizes)[None, :])
    return order + jnp.sum(jnp.where(inside, shift[None, :], 0), axis=1)


def on_device(draft_rows, tree_sizes, draft_map, row_order, up_weight, down_weight):
    own, width = draft_rows.shape
    rows, hidden_units = row_order.shape[0], up_weight.shape[1]
    part = hidden_units // 4
    g, gc, dr = lax.axis_index("gr"), lax.axis_index("gc"), lax.axis_index("dr")
    chip, core = g >> 1, g & 1
    bits = square_bits(gc >> 1) + square_bits(dr * 2 + (gc & 1))

    pair = jnp.concatenate([draft_rows, other_core(draft_rows)])
    gathered = jnp.concatenate([pair] + [from_chip(pair, ahead) for ahead in (1, 3, 2)])

    order = row_order.reshape(2, 2, 2, 2, rows // 16)
    for axis in range(4):
        order = jnp.where(bits[axis] == 1, jnp.flip(order, axis), order)
    source = source_rows(tree_sizes, draft_map, order.reshape(rows))
    ahead = ((source // (2 * own)) - chip) & 3
    slot = jnp.where(ahead == 2, 3, jnp.where(ahead == 3, 2, ahead))
    at = (slot * 2 + (((source // own) & 1) ^ core)) * own + source % own
    places = jnp.arange(rows, dtype=jnp.int32)
    pick = (at[:, None] == places[None, :]).astype(BF)
    candidates = jnp.dot(pick, gathered, preferred_element_type=F32).astype(BF)
    cube = candidates.reshape(2, 2, 2, 2, rows // 16, width)

    def half(value, axis, which):
        return lax.index_in_dim(value, which, axis, keepdims=False)

    def flat(value):
        return value.reshape(-1, value.shape[-1])

    total = []
    for q in range(4):
        sides = [(q + i) % 4 for i in range(4)]
        left = list(range(4))
        up = up_weight[:, q * part : (q + 1) * part]
        down = down_weight[q * part : (q + 1) * part]

        def project(which):
            lhs = half(cube, q, which)
            value = jnp.dot(flat(lhs), up, preferred_element_type=F32)
            return value.reshape(lhs.shape[:-1] + (part,))

        value = None
        for i, side in enumerate(sides):
            axis = left.index(side)
            if i == 0:
                sent, kept = project(1), project(0)
            elif i < RS_STEPS:
                sent, kept = half(value, axis, 1), half(value, axis, 0)
            else:
                sent, kept = jnp.flip(value, axis), value
            value = kept + swap(sent.astype(BF), side).astype(F32)
            if i < RS_STEPS:
                left.remove(side)
        value = jax.nn.gelu(value, approximate=False).astype(BF)
        for side in reversed(sides[1:RS_STEPS]):
            left = sorted(left + [side])
            value = jnp.stack([value, swap(value, side)], axis=left.index(side))
        other = swap(value, sides[0])
        outs = [
            jnp.dot(flat(v), down, preferred_element_type=F32).reshape(v.shape[:-1] + (width,))
            for v in (value, other)
        ]
        total.append(jnp.stack(outs, axis=q))
    total = (total[0] + total[1]) + (total[2] + total[3])

    spot = places
    target = ((((spot // (2 * own)) + chip) & 3) * 2 + (((spot // own) & 1) ^ core)) * own + spot % own
    mask = ((bits[0] * 2 + bits[1]) * 2 + bits[2]) * 2 + bits[3]
    local = target ^ (mask * (rows // 16))
    pick_out = (local[:, None] == places[None, :]).astype(BF)
    result = jnp.dot(pick_out, total.reshape(rows, width).astype(BF), preferred_element_type=F32)
    result = result.reshape(4, 2, own, width)
    result = result[:, 0] + other_core(result[:, 1].astype(BF)).astype(F32)
    mine = result[0]
    for ahead in (1, 3, 2):
        mine = mine + from_chip(result[(4 - ahead) % 4].astype(BF), ahead).astype(F32)
    return mine.astype(BF)


def solution(mesh):
    return jax.shard_map(
        on_device,
        mesh=mesh,
        in_specs=(
            P("gr", ("gc", "dr")),
            P(),
            P(),
            P(),
            P(("gc", "dr"), "gr"),
            P("gr", ("gc", "dr")),
        ),
        out_specs=P("gr", ("gc", "dr")),
        check_vma=False,
    )
```

```python
import functools

import jax
import jax.numpy as jnp
from jax import lax
from jax.experimental import pallas as pl
from jax.experimental.pallas import tpu as pltpu
from jax.sharding import PartitionSpec as P

BF, F32 = jnp.bfloat16, jnp.float32
YZ = ("gc", "dr")
LIMIT = 8 << 20


def place(y, z):
    return (y * 2 + z % 2) * 2 + z // 2


SIDES = ((1, 0, 3, 2), (3, 2, 1, 0))
SWAPS = tuple(
    [(place(y, z), place(side[y], z)) for y in range(4) for z in range(4)] for side in SIDES
) + tuple(
    [(place(y, z), place(y, side[z])) for y in range(4) for z in range(4)] for side in SIDES
)


def swap(value, side):
    return lax.ppermute(value, YZ, SWAPS[side])


def from_chip(value, ahead):
    pairs = [(((x + ahead) % 4) * 2 + c, x * 2 + c) for x in range(4) for c in range(2)]
    return lax.ppermute(value, "gr", pairs)


def other_core(value):
    return lax.ppermute(value, "gr", [(i, i ^ 1) for i in range(8)])


def square_bits(p):
    return (p & 1) ^ (p >> 1), p >> 1


def run(kernel, outs, *args, spaces=None, flops=0, moved=0, erfs=0, aliases=None, scratch=()):
    vmem = pl.BlockSpec(memory_space=pltpu.VMEM)
    specs = [vmem] * len(args)
    for i, space in (spaces or {}).items():
        specs[i] = pl.BlockSpec(memory_space=space)
    single = not isinstance(outs, list)
    shapes = [outs] if single else outs
    moved = moved or sum(a.size * a.dtype.itemsize for a in args)
    out = pl.pallas_call(
        kernel,
        out_shape=shapes,
        in_specs=specs,
        out_specs=[vmem] * len(shapes),
        scratch_shapes=list(scratch),
        input_output_aliases=aliases or {},
        compiler_params=pltpu.CompilerParams(vmem_limit_bytes=LIMIT),
        cost_estimate=pl.CostEstimate(flops=flops, bytes_accessed=moved, transcendentals=erfs),
    )(*args)
    return out[0] if single else out


def load_kernel(count, *refs):
    src, extras = refs[0], refs[1 : 1 + count]
    out, extra_outs, sems = refs[-2 - count], refs[-1 - count : -1], refs[-1]
    width = out.shape[2]
    copies = [
        pltpu.make_async_copy(src.at[:, pl.ds(i * width, width)], out.at[i], sems.at[i])
        for i in range(4)
    ]
    for i in range(count):
        copies.append(pltpu.make_async_copy(extras[i], extra_outs[i], sems.at[4 + i]))
    for copy in copies:
        copy.start()
    for copy in copies:
        copy.wait()


def load(weight, *extras, after=None):
    rows, columns = weight.shape
    count = len(extras)
    values = [pltpu.with_memory_space_constraint(v, pltpu.HBM) for v in (weight, *extras)]
    spaces = {i: pltpu.HBM for i in range(1 + count)}
    if after is not None:
        values.append(after)
        spaces[1 + count] = pl.ANY
    out = run(
        functools.partial(load_kernel, count),
        [pltpu.VMEM((4, rows, columns // 4), BF)] + [pltpu.VMEM(v.shape, v.dtype) for v in extras],
        *values,
        spaces=spaces,
        moved=weight.size * 4,
        scratch=[pltpu.SemaphoreType.DMA((4 + count,))],
    )
    return out if extras else out[0]


def pack_kernel(*refs):
    out, at = refs[-1], 0
    for ref in refs[:-1]:
        out[at : at + ref.shape[0]] = ref[...]
        at += ref.shape[0]


def pack(*values):
    rows = sum(v.shape[0] for v in values)
    return run(pack_kernel, pltpu.VMEM((rows, values[0].shape[1]), BF), *values)


def side_bit(ids, side):
    return (square_bits(ids[1] >> 1) + square_bits(ids[2] * 2 + (ids[1] & 1)))[side % 4]


def quarter_of(ids, q, far):
    return (q % 2) * 2 + (side_bit(ids, q) ^ far)


def half_of(ids, q, near, rows):
    return pl.ds(pl.multiple_of((side_bit(ids, q + 1) ^ near) * rows, rows), rows)


def up_kernel(q, far, ids, rows_ref, weight_ref, after, out_ref):
    half = out_ref.shape[0] // 2
    rows = jnp.concatenate([rows_ref[half_of(ids, q, near, half)] for near in range(2)])
    quarter = quarter_of(ids, q, far)
    width = weight_ref.shape[2]
    for start in range(0, width, 256):
        stop = min(start + 256, width)
        value = jnp.dot(rows, weight_ref[quarter, :, start:stop], preferred_element_type=F32)
        out_ref[:, start:stop] = value.astype(out_ref.dtype)


def second_kernel(kept_ref, got_ref, after, out_ref):
    n = out_ref.shape[0]
    out_ref[...] = (kept_ref[n:] + got_ref[n:].astype(F32)).astype(BF)


def third_kernel(kept_ref, got_ref, new_ref, sum_ref, out_ref):
    n = out_ref.shape[0]
    value = kept_ref[:n] + got_ref[:n].astype(F32) + new_ref[...].astype(F32)
    sum_ref[...] = value
    out_ref[...] = value.astype(BF)


def fourth_kernel(kept_ref, got_ref, sum_ref, out_ref):
    value = kept_ref[...] + got_ref[...].astype(F32)
    sum_ref[...] = value
    out_ref[...] = value.astype(BF)


def gelu_kernel(kept_ref, got_ref, out_ref):
    value = kept_ref[...] + got_ref[...].astype(F32)
    value = value * (1.0 + lax.erf(value * (2.0**-0.5))) * 0.5
    out_ref[...] = value.astype(BF)


def add_down(ids, q, far, rows_ref, weight_ref, from_ref, out_ref):
    half = out_ref.shape[0] // 2
    value = lax.dot_general(
        rows_ref[...],
        weight_ref[quarter_of(ids, q, far)],
        (((1,), (1,)), ((), ())),
        preferred_element_type=F32,
    )
    for near in range(2):
        at = half_of(ids, q, near, half)
        rows = value[near * half : (near + 1) * half]
        out_ref[at] = rows if from_ref is None else from_ref[at] + rows


def down_own_kernel(q, ids, one_ref, two_ref, weight_ref, out_ref):
    add_down(ids, q, 0, one_ref, weight_ref, None, out_ref)
    add_down(ids, q + 1, 0, two_ref, weight_ref, out_ref, out_ref)


def down_kernel(q, ids, total_ref, rows_ref, weight_ref, out_ref):
    add_down(ids, q, 1, rows_ref, weight_ref, total_ref, out_ref)


def index_kernel(ids, sizes_ref, map_ref, order_ref, after, out_ref, mid_ref):
    rows = order_ref.shape[1]
    reqs = sizes_ref.shape[1]
    own = rows // 8
    down_at = lax.broadcasted_iota(jnp.int32, (reqs, reqs), 0)
    along = lax.broadcasted_iota(jnp.int32, (reqs, reqs), 1)
    sizes, owner = sizes_ref[...], map_ref[...]

    def upright(row):
        return jnp.sum(jnp.where(down_at == along, row, 0), axis=1, keepdims=True)

    earlier = along < down_at
    owners = upright(owner)
    before = (owner < owners) | ((owner == owners) & earlier)
    start = jnp.sum(jnp.where(earlier, sizes, 0), axis=1, keepdims=True)
    shift = jnp.sum(jnp.where(before, sizes, 0), axis=1, keepdims=True) - start
    order = order_ref[...]
    inside = (order >= start) & (order < start + upright(sizes))
    source = order + jnp.sum(jnp.where(inside, shift, 0), axis=0, keepdims=True)
    chip, core = ids[0] >> 1, ids[0] & 1
    ahead = (source // (2 * own) - chip) & 3
    slot = jnp.where(ahead == 2, 1, jnp.where(ahead == 1, 2, ahead))
    at = (((source // own) & 1) ^ core) * (4 * own) + slot * own + source % own
    spots = lax.broadcasted_iota(jnp.int32, (rows, rows), 0)
    mid_ref[...] = jnp.where(spots == at, 1.0, 0.0).T.astype(BF)
    for t in range(8):
        block = ((t + chip) & 3) * 2 + ((t // 4) ^ core)
        out_ref[t * own : (t + 1) * own] = mid_ref[pl.ds(pl.multiple_of(block * own, own), own)]


def sort_kernel(at, pick_ref, value_ref, *refs):
    kept_ref, out_ref = refs[-2:]
    half = kept_ref.shape[0]
    value = value_ref[...]
    high = value.astype(BF)
    low = (value - high.astype(F32)).astype(BF)
    pick = pick_ref[:, at : at + value.shape[0]]
    kept = jnp.dot(pick[:half], high, preferred_element_type=F32)
    kept += jnp.dot(pick[:half], low, preferred_element_type=F32)
    out = jnp.dot(pick[half:], high, preferred_element_type=F32)
    if len(refs) == 4:
        kept += refs[0][...]
        out += refs[1][...]
    kept_ref[...] = kept
    out_ref[...] = out.astype(out_ref.dtype)


def deal_kernel(kept_ref, got_ref, mine_ref, *out_refs):
    n = mine_ref.shape[0]
    mine_ref[...] = kept_ref[:n] + got_ref[:n].astype(F32)
    for i, out_ref in enumerate(out_refs):
        at = slice((i + 1) * n, (i + 2) * n)
        out_ref[...] = (kept_ref[at] + got_ref[at].astype(F32)).astype(BF)


def last_kernel(mine_ref, *refs):
    value = mine_ref[...]
    for ref in refs[:-1]:
        value += ref[...].astype(F32)
    refs[-1][...] = value.astype(BF)


def on_device(draft_rows, tree_sizes, draft_map, row_order, up_weight, down_weight):
    own, width = draft_rows.shape
    rows, hidden_units = row_order.shape[0], up_weight.shape[1]
    part = hidden_units // 4
    group = rows // 2
    chains = range(4)
    ids = jnp.stack([lax.axis_index("gr"), lax.axis_index("gc"), lax.axis_index("dr")])
    ids = ids.astype(jnp.int32)
    smem = pltpu.SMEM

    fetched = [from_chip(draft_rows, ahead) for ahead in (2, 1, 3)]
    ups, draft = load(up_weight, draft_rows)
    column = pack(draft, *fetched)
    beside = other_core(column)

    project_flops = 2 * group * width * part

    def project(q, far, dtype, after):
        return run(
            functools.partial(up_kernel, q, far),
            pltpu.VMEM((group, part), dtype),
            ids,
            column if q < 2 else beside,
            ups,
            after,
            spaces={0: smem, 3: pl.ANY},
            flops=project_flops,
        )

    sent, after = [], column
    for q in chains:
        after = project(q, 1, BF, after)
        sent.append(after)
    got = [swap(sent[q], q) for q in chains]
    kept = []
    for q in chains:
        after = project(q, 0, F32, after)
        kept.append(after)
    pick = run(
        index_kernel,
        pltpu.VMEM((rows, rows), BF),
        ids,
        tree_sizes[None, :],
        draft_map[None, :],
        row_order[None, :],
        after,
        spaces={0: smem, 4: pl.ANY},
        flops=rows * rows * 64,
        scratch=[pltpu.VMEM((rows, rows), BF)],
    )
    downs = load(down_weight.T, after=after)

    block = pltpu.VMEM((group // 2, part), BF)
    block32 = pltpu.VMEM((group // 2, part), F32)
    came = [
        swap(run(second_kernel, block, kept[q], got[q], after, spaces={2: pl.ANY}), (q + 1) % 4)
        for q in chains
    ]
    third = [run(third_kernel, [block32, block], kept[q], got[q], came[q]) for q in chains]
    came = [swap(third[q][1], (q + 2) % 4) for q in chains]
    fourth = [run(fourth_kernel, [block32, block], third[q][0], came[q]) for q in chains]
    came = [swap(fourth[q][1], (q + 3) % 4) for q in chains]
    erfs = group // 2 * part
    hidden = [run(gelu_kernel, block, fourth[q][0], came[q], erfs=erfs) for q in chains]
    came = [swap(hidden[q], (q + 1) % 4) for q in chains]
    mine = [pack(hidden[q], came[q]) for q in chains]
    came = [swap(mine[q], q) for q in chains]
    whole = pltpu.VMEM((group, width), F32)
    sorted_rows = []
    for i in range(2):
        total = run(
            functools.partial(down_own_kernel, 2 * i),
            whole,
            ids,
            mine[2 * i],
            mine[2 * i + 1],
            downs,
            spaces={0: smem},
            flops=2 * project_flops,
        )
        for q in (2 * i, 2 * i + 1):
            total = run(
                functools.partial(down_kernel, q),
                whole,
                ids,
                total,
                came[q],
                downs,
                spaces={0: smem},
                flops=project_flops,
            )
        sorted_rows = run(
            functools.partial(sort_kernel, i * group),
            [whole, pltpu.VMEM((group, width), BF if i else F32)],
            pick,
            total,
            *sorted_rows,
            flops=3 * group * group * width,
        )
    kept, out = sorted_rows
    row_block = pltpu.VMEM((own, width), BF)
    mine, one, two, three = run(
        deal_kernel,
        [pltpu.VMEM((own, width), F32), row_block, row_block, row_block],
        kept,
        other_core(out),
    )
    arrived = [from_chip(value, ahead) for ahead, value in ((2, two), (1, three), (3, one))]
    return run(last_kernel, jax.ShapeDtypeStruct((own, width), BF), mine, *arrived)


def solution(mesh):
    return jax.shard_map(
        on_device,
        mesh=mesh,
        in_specs=(
            P("gr", ("gc", "dr")),
            P(),
            P(),
            P(),
            P(("gc", "dr"), "gr"),
            P("gr", ("gc", "dr")),
        ),
        out_specs=P("gr", ("gc", "dr")),
        check_vma=False,
    )
```

```python
import functools

import jax
import jax.numpy as jnp
from jax import lax
from jax.experimental import pallas as pl
from jax.experimental.pallas import tpu as pltpu
from jax.sharding import PartitionSpec as P

BF, F32 = jnp.bfloat16, jnp.float32
YZ = ("gc", "dr")
LIMIT = 8 << 20


def place(y, z):
    return (y * 2 + z % 2) * 2 + z // 2


SIDES = ((1, 0, 3, 2), (3, 2, 1, 0))
SWAPS = tuple(
    [(place(y, z), place(side[y], z)) for y in range(4) for z in range(4)] for side in SIDES
) + tuple(
    [(place(y, z), place(y, side[z])) for y in range(4) for z in range(4)] for side in SIDES
)


def swap(value, side):
    return lax.ppermute(value, YZ, SWAPS[side])


def from_chip(value, ahead):
    pairs = [(((x + ahead) % 4) * 2 + c, x * 2 + c) for x in range(4) for c in range(2)]
    return lax.ppermute(value, "gr", pairs)


def other_core(value):
    return lax.ppermute(value, "gr", [(i, i ^ 1) for i in range(8)])


def square_bits(p):
    return (p & 1) ^ (p >> 1), p >> 1


def run(kernel, outs, *args, spaces=None, flops=0, moved=0, erfs=0, aliases=None, scratch=()):
    vmem = pl.BlockSpec(memory_space=pltpu.VMEM)
    specs = [vmem] * len(args)
    for i, space in (spaces or {}).items():
        specs[i] = pl.BlockSpec(memory_space=space)
    single = not isinstance(outs, list)
    shapes = [outs] if single else outs
    moved = moved or sum(a.size * a.dtype.itemsize for a in args)
    out = pl.pallas_call(
        kernel,
        out_shape=shapes,
        in_specs=specs,
        out_specs=[vmem] * len(shapes),
        scratch_shapes=list(scratch),
        input_output_aliases=aliases or {},
        compiler_params=pltpu.CompilerParams(vmem_limit_bytes=LIMIT),
        cost_estimate=pl.CostEstimate(flops=flops, bytes_accessed=moved, transcendentals=erfs),
    )(*args)
    return out[0] if single else out


def load_kernel(count, *refs):
    src, extras = refs[0], refs[1 : 1 + count]
    out, extra_outs, sems = refs[-2 - count], refs[-1 - count : -1], refs[-1]
    width = out.shape[2]
    copies = [
        pltpu.make_async_copy(src.at[:, pl.ds(i * width, width)], out.at[i], sems.at[i])
        for i in range(4)
    ]
    for i in range(count):
        copies.append(pltpu.make_async_copy(extras[i], extra_outs[i], sems.at[4 + i]))
    for copy in copies:
        copy.start()
    for copy in copies:
        copy.wait()


def load(weight, *extras, after=None):
    rows, columns = weight.shape
    count = len(extras)
    values = [pltpu.with_memory_space_constraint(v, pltpu.HBM) for v in (weight, *extras)]
    spaces = {i: pltpu.HBM for i in range(1 + count)}
    if after is not None:
        values.append(after)
        spaces[1 + count] = pl.ANY
    out = run(
        functools.partial(load_kernel, count),
        [pltpu.VMEM((4, rows, columns // 4), BF)] + [pltpu.VMEM(v.shape, v.dtype) for v in extras],
        *values,
        spaces=spaces,
        moved=weight.size * 4,
        scratch=[pltpu.SemaphoreType.DMA((4 + count,))],
    )
    return out if extras else out[0]


def pack_kernel(*refs):
    out, at = refs[-1], 0
    for ref in refs[:-1]:
        out[at : at + ref.shape[0]] = ref[...]
        at += ref.shape[0]


def pack(*values):
    rows = sum(v.shape[0] for v in values)
    return run(pack_kernel, pltpu.VMEM((rows, values[0].shape[1]), BF), *values)


def side_bit(side):
    gc = lax.axis_index("gc")
    if side % 4 < 2:
        return square_bits(gc >> 1)[side % 4]
    return square_bits(lax.axis_index("dr") * 2 + (gc & 1))[side % 4 - 2]


def quarter_of(q, far):
    return (q % 2) * 2 + (side_bit(q) ^ far)


def half_of(q, near, rows):
    return pl.ds(pl.multiple_of((side_bit(q + 1) ^ near) * rows, rows), rows)


def up_kernel(q, far, rows_ref, weight_ref, after, out_ref):
    half = out_ref.shape[0] // 2
    rows = jnp.concatenate([rows_ref[half_of(q, near, half)] for near in range(2)])
    quarter = quarter_of(q, far)
    width = weight_ref.shape[2]
    for start in range(0, width, 256):
        stop = min(start + 256, width)
        value = jnp.dot(rows, weight_ref[quarter, :, start:stop], preferred_element_type=F32)
        out_ref[:, start:stop] = value.astype(out_ref.dtype)


def second_kernel(kept_ref, got_ref, after, out_ref):
    n = out_ref.shape[0]
    out_ref[...] = (kept_ref[n:] + got_ref[n:].astype(F32)).astype(BF)


def third_kernel(kept_ref, got_ref, new_ref, sum_ref, out_ref):
    n = out_ref.shape[0]
    value = kept_ref[:n] + got_ref[:n].astype(F32) + new_ref[...].astype(F32)
    sum_ref[...] = value
    out_ref[...] = value.astype(BF)


def fourth_kernel(kept_ref, got_ref, sum_ref, out_ref):
    value = kept_ref[...] + got_ref[...].astype(F32)
    sum_ref[...] = value
    out_ref[...] = value.astype(BF)


def gelu_kernel(kept_ref, got_ref, out_ref):
    value = kept_ref[...] + got_ref[...].astype(F32)
    value = value * (1.0 + lax.erf(value * (2.0**-0.5))) * 0.5
    out_ref[...] = value.astype(BF)


def add_down(q, far, rows_ref, weight_ref, from_ref, out_ref):
    half = out_ref.shape[0] // 2
    value = lax.dot_general(
        rows_ref[...],
        weight_ref[quarter_of(q, far)],
        (((1,), (1,)), ((), ())),
        preferred_element_type=F32,
    )
    for near in range(2):
        at = half_of(q, near, half)
        rows = value[near * half : (near + 1) * half]
        out_ref[at] = rows if from_ref is None else from_ref[at] + rows


def down_own_kernel(q, one_ref, two_ref, weight_ref, out_ref):
    add_down(q, 0, one_ref, weight_ref, None, out_ref)
    add_down(q + 1, 0, two_ref, weight_ref, out_ref, out_ref)


def down_kernel(q, total_ref, rows_ref, weight_ref, out_ref):
    add_down(q, 1, rows_ref, weight_ref, total_ref, out_ref)


def index_kernel(sizes_ref, map_ref, order_ref, after, out_ref, mid_ref):
    rows = order_ref.shape[1]
    reqs = sizes_ref.shape[1]
    own = rows // 8
    down_at = lax.broadcasted_iota(jnp.int32, (reqs, reqs), 0)
    along = lax.broadcasted_iota(jnp.int32, (reqs, reqs), 1)
    sizes, owner = sizes_ref[...], map_ref[...]

    def upright(row):
        return jnp.sum(jnp.where(down_at == along, row, 0), axis=1, keepdims=True)

    earlier = along < down_at
    owners = upright(owner)
    before = (owner < owners) | ((owner == owners) & earlier)
    start = jnp.sum(jnp.where(earlier, sizes, 0), axis=1, keepdims=True)
    shift = jnp.sum(jnp.where(before, sizes, 0), axis=1, keepdims=True) - start
    order = order_ref[...]
    inside = (order >= start) & (order < start + upright(sizes))
    source = order + jnp.sum(jnp.where(inside, shift, 0), axis=0, keepdims=True)
    g = lax.axis_index("gr")
    chip, core = g >> 1, g & 1
    ahead = (source // (2 * own) - chip) & 3
    slot = jnp.where(ahead == 2, 1, jnp.where(ahead == 1, 2, ahead))
    at = (((source // own) & 1) ^ core) * (4 * own) + slot * own + source % own
    spots = lax.broadcasted_iota(jnp.int32, (rows, rows), 0)
    mid_ref[...] = jnp.where(spots == at, 1.0, 0.0).T.astype(BF)
    for t in range(8):
        block = ((t + chip) & 3) * 2 + ((t // 4) ^ core)
        out_ref[t * own : (t + 1) * own] = mid_ref[pl.ds(pl.multiple_of(block * own, own), own)]


def sort_kernel(at, pick_ref, value_ref, *refs):
    kept_ref, out_ref = refs[-2:]
    half = kept_ref.shape[0]
    value = value_ref[...]
    high = value.astype(BF)
    low = (value - high.astype(F32)).astype(BF)
    pick = pick_ref[:, at : at + value.shape[0]]
    kept = jnp.dot(pick[:half], high, preferred_element_type=F32)
    kept += jnp.dot(pick[:half], low, preferred_element_type=F32)
    out = jnp.dot(pick[half:], high, preferred_element_type=F32)
    if len(refs) == 4:
        kept += refs[0][...]
        out += refs[1][...]
    kept_ref[...] = kept
    out_ref[...] = out.astype(out_ref.dtype)


def deal_kernel(kept_ref, got_ref, mine_ref, *out_refs):
    n = mine_ref.shape[0]
    mine_ref[...] = kept_ref[:n] + got_ref[:n].astype(F32)
    for i, out_ref in enumerate(out_refs):
        at = slice((i + 1) * n, (i + 2) * n)
        out_ref[...] = (kept_ref[at] + got_ref[at].astype(F32)).astype(BF)


def last_kernel(mine_ref, *refs):
    value = mine_ref[...]
    for ref in refs[:-1]:
        value += ref[...].astype(F32)
    refs[-1][...] = value.astype(BF)


def on_device(draft_rows, tree_sizes, draft_map, row_order, up_weight, down_weight):
    own, width = draft_rows.shape
    rows, hidden_units = row_order.shape[0], up_weight.shape[1]
    part = hidden_units // 4
    group = rows // 2
    chains = range(4)

    fetched = [from_chip(draft_rows, ahead) for ahead in (2, 1, 3)]
    ups, draft = load(up_weight, draft_rows)
    column = pack(draft, *fetched)
    beside = other_core(column)

    project_flops = 2 * group * width * part

    def project(q, far, dtype, after):
        return run(
            functools.partial(up_kernel, q, far),
            pltpu.VMEM((group, part), dtype),
            column if q < 2 else beside,
            ups,
            after,
            spaces={2: pl.ANY},
            flops=project_flops,
        )

    sent, after = [], column
    for q in chains:
        after = project(q, 1, BF, after)
        sent.append(after)
    got = [swap(sent[q], q) for q in chains]
    kept = []
    for q in chains:
        after = project(q, 0, F32, after)
        kept.append(after)
    pick = run(
        index_kernel,
        pltpu.VMEM((rows, rows), BF),
        tree_sizes[None, :],
        draft_map[None, :],
        row_order[None, :],
        after,
        spaces={3: pl.ANY},
        flops=rows * rows * 64,
        scratch=[pltpu.VMEM((rows, rows), BF)],
    )
    downs = load(down_weight.T, after=after)

    block = pltpu.VMEM((group // 2, part), BF)
    block32 = pltpu.VMEM((group // 2, part), F32)
    came = [
        swap(run(second_kernel, block, kept[q], got[q], after, spaces={2: pl.ANY}), (q + 1) % 4)
        for q in chains
    ]
    third = [run(third_kernel, [block32, block], kept[q], got[q], came[q]) for q in chains]
    came = [swap(third[q][1], (q + 2) % 4) for q in chains]
    fourth = [run(fourth_kernel, [block32, block], third[q][0], came[q]) for q in chains]
    came = [swap(fourth[q][1], (q + 3) % 4) for q in chains]
    erfs = group // 2 * part
    hidden = [run(gelu_kernel, block, fourth[q][0], came[q], erfs=erfs) for q in chains]
    came = [swap(hidden[q], (q + 1) % 4) for q in chains]
    mine = [pack(hidden[q], came[q]) for q in chains]
    came = [swap(mine[q], q) for q in chains]
    whole = pltpu.VMEM((group, width), F32)
    sorted_rows = []
    for i in range(2):
        total = run(
            functools.partial(down_own_kernel, 2 * i),
            whole,
            mine[2 * i],
            mine[2 * i + 1],
            downs,
            flops=2 * project_flops,
        )
        for q in (2 * i, 2 * i + 1):
            total = run(
                functools.partial(down_kernel, q),
                whole,
                    total,
                came[q],
                downs,
                    flops=project_flops,
            )
        sorted_rows = run(
            functools.partial(sort_kernel, i * group),
            [whole, pltpu.VMEM((group, width), BF if i else F32)],
            pick,
            total,
            *sorted_rows,
            flops=3 * group * group * width,
        )
    kept, out = sorted_rows
    row_block = pltpu.VMEM((own, width), BF)
    mine, one, two, three = run(
        deal_kernel,
        [pltpu.VMEM((own, width), F32), row_block, row_block, row_block],
        kept,
        other_core(out),
    )
    arrived = [from_chip(value, ahead) for ahead, value in ((2, two), (1, three), (3, one))]
    return run(last_kernel, jax.ShapeDtypeStruct((own, width), BF), mine, *arrived)


def solution(mesh):
    return jax.shard_map(
        on_device,
        mesh=mesh,
        in_specs=(
            P("gr", ("gc", "dr")),
            P(),
            P(),
            P(),
            P(("gc", "dr"), "gr"),
            P("gr", ("gc", "dr")),
        ),
        out_specs=P("gr", ("gc", "dr")),
        check_vma=False,
    )
```

```python
import functools

import jax
import jax.numpy as jnp
from jax import lax
from jax.experimental import pallas as pl
from jax.experimental.pallas import tpu as pltpu
from jax.sharding import PartitionSpec as P

BF, F32 = jnp.bfloat16, jnp.float32
YZ = ("gc", "dr")
LIMIT = 8 << 20


def place(y, z):
    return (y * 2 + z % 2) * 2 + z // 2


SIDES = ((1, 0, 3, 2), (3, 2, 1, 0))
SWAPS = tuple(
    [(place(y, z), place(side[y], z)) for y in range(4) for z in range(4)] for side in SIDES
) + tuple(
    [(place(y, z), place(y, side[z])) for y in range(4) for z in range(4)] for side in SIDES
)


def swap(value, side):
    return lax.ppermute(value, YZ, SWAPS[side])


def from_chip(value, ahead):
    pairs = [(((x + ahead) % 4) * 2 + c, x * 2 + c) for x in range(4) for c in range(2)]
    return lax.ppermute(value, "gr", pairs)


def other_core(value):
    return lax.ppermute(value, "gr", [(i, i ^ 1) for i in range(8)])


def square_bits(p):
    return (p & 1) ^ (p >> 1), p >> 1


class Line:
    def __init__(self):
        self.last = None

    def __call__(self, kernel, outs, *args, after=(), spaces=None, flops=0, moved=0, erfs=0, scratch=()):
        waits = [*after] if self.last is None else [self.last, *after]
        vmem = pl.BlockSpec(memory_space=pltpu.VMEM)
        specs = [vmem] * len(args) + [pl.BlockSpec(memory_space=pl.ANY)] * len(waits)
        for i, space in (spaces or {}).items():
            specs[i] = pl.BlockSpec(memory_space=space)
        single = not isinstance(outs, list)
        shapes = [outs] if single else outs
        moved = moved or sum(a.size * a.dtype.itemsize for a in args)

        def body(*refs):
            kernel(*refs[: len(args)], *refs[len(args) + len(waits) :])

        out = pl.pallas_call(
            body,
            out_shape=shapes,
            in_specs=specs,
            out_specs=[vmem] * len(shapes),
            scratch_shapes=list(scratch),
            compiler_params=pltpu.CompilerParams(vmem_limit_bytes=LIMIT),
            cost_estimate=pl.CostEstimate(flops=flops, bytes_accessed=moved, transcendentals=erfs),
        )(*args, *waits)
        self.last = out[0]
        return out[0] if single else out


def load_kernel(count, *refs):
    src, extras = refs[0], refs[1 : 1 + count]
    out, extra_outs, sems = refs[-2 - count], refs[-1 - count : -1], refs[-1]
    width = out.shape[2]
    copies = [
        pltpu.make_async_copy(src.at[:, pl.ds(i * width, width)], out.at[i], sems.at[i])
        for i in range(4)
    ]
    for i in range(count):
        copies.append(pltpu.make_async_copy(extras[i], extra_outs[i], sems.at[4 + i]))
    for copy in copies:
        copy.start()
    for copy in copies:
        copy.wait()


def load(run, weight, *extras):
    rows, columns = weight.shape
    count = len(extras)
    values = [pltpu.with_memory_space_constraint(v, pltpu.HBM) for v in (weight, *extras)]
    out = run(
        functools.partial(load_kernel, count),
        [pltpu.VMEM((4, rows, columns // 4), BF)] + [pltpu.VMEM(v.shape, v.dtype) for v in extras],
        *values,
        spaces={i: pltpu.HBM for i in range(1 + count)},
        moved=weight.size * 4,
        scratch=[pltpu.SemaphoreType.DMA((4 + count,))],
    )
    return out if extras else out[0]


def pack_kernel(*refs):
    out, at = refs[-1], 0
    for ref in refs[:-1]:
        out[at : at + ref.shape[0]] = ref[...]
        at += ref.shape[0]


def pack(run, *values):
    rows = sum(v.shape[0] for v in values)
    return run(pack_kernel, pltpu.VMEM((rows, values[0].shape[1]), BF), *values)


def copied(run, value, *after):
    return run(pack_kernel, pltpu.VMEM(value.shape, value.dtype), value, after=after)


def side_bit(side):
    gc = lax.axis_index("gc")
    if side % 4 < 2:
        return square_bits(gc >> 1)[side % 4]
    return square_bits(lax.axis_index("dr") * 2 + (gc & 1))[side % 4 - 2]


def quarter_of(q, far):
    return (q % 2) * 2 + (side_bit(q) ^ far)


def half_of(q, near, rows):
    return pl.ds(pl.multiple_of((side_bit(q + 1) ^ near) * rows, rows), rows)


def up_kernel(q, far, rows_ref, weight_ref, out_ref):
    half = out_ref.shape[0] // 2
    rows = jnp.concatenate([rows_ref[half_of(q, near, half)] for near in range(2)])
    quarter = quarter_of(q, far)
    width = weight_ref.shape[2]
    for start in range(0, width, 256):
        stop = min(start + 256, width)
        value = jnp.dot(rows, weight_ref[quarter, :, start:stop], preferred_element_type=F32)
        out_ref[:, start:stop] = value.astype(out_ref.dtype)


def second_kernel(kept_ref, got_ref, out_ref):
    n = out_ref.shape[0]
    out_ref[...] = (kept_ref[n:] + got_ref[n:].astype(F32)).astype(BF)


def third_kernel(kept_ref, got_ref, new_ref, sum_ref, out_ref):
    n = out_ref.shape[0]
    value = kept_ref[:n] + got_ref[:n].astype(F32) + new_ref[...].astype(F32)
    sum_ref[...] = value
    out_ref[...] = value.astype(BF)


def fourth_kernel(kept_ref, got_ref, sum_ref, out_ref):
    value = kept_ref[...] + got_ref[...].astype(F32)
    sum_ref[...] = value
    out_ref[...] = value.astype(BF)


def gelu_kernel(kept_ref, got_ref, out_ref):
    value = kept_ref[...] + got_ref[...].astype(F32)
    value = value * (1.0 + lax.erf(value * (2.0**-0.5))) * 0.5
    out_ref[...] = value.astype(BF)


def add_down(q, far, near_ref, far_ref, weight_ref, from_ref, out_ref):
    half = out_ref.shape[0] // 2
    value = lax.dot_general(
        jnp.concatenate([near_ref[...], far_ref[...]]),
        weight_ref[quarter_of(q, far)],
        (((1,), (1,)), ((), ())),
        preferred_element_type=F32,
    )
    for near in range(2):
        at = half_of(q, near, half)
        rows = value[near * half : (near + 1) * half]
        out_ref[at] = rows if from_ref is None else from_ref[at] + rows


def down_own_kernel(q, one, one_more, two, two_more, weight_ref, out_ref):
    add_down(q, 0, one, one_more, weight_ref, None, out_ref)
    add_down(q + 1, 0, two, two_more, weight_ref, out_ref, out_ref)


def down_kernel(q, total_ref, near_ref, far_ref, weight_ref, out_ref):
    add_down(q, 1, near_ref, far_ref, weight_ref, total_ref, out_ref)


def index_kernel(sizes_ref, map_ref, order_ref, out_ref, mid_ref):
    rows = order_ref.shape[1]
    reqs = sizes_ref.shape[1]
    own = rows // 8
    down_at = lax.broadcasted_iota(jnp.int32, (reqs, reqs), 0)
    along = lax.broadcasted_iota(jnp.int32, (reqs, reqs), 1)
    sizes, owner = sizes_ref[...], map_ref[...]

    def upright(row):
        return jnp.sum(jnp.where(down_at == along, row, 0), axis=1, keepdims=True)

    earlier = along < down_at
    owners = upright(owner)
    before = (owner < owners) | ((owner == owners) & earlier)
    start = jnp.sum(jnp.where(earlier, sizes, 0), axis=1, keepdims=True)
    shift = jnp.sum(jnp.where(before, sizes, 0), axis=1, keepdims=True) - start
    order = order_ref[...]
    inside = (order >= start) & (order < start + upright(sizes))
    source = order + jnp.sum(jnp.where(inside, shift, 0), axis=0, keepdims=True)
    g = lax.axis_index("gr")
    chip, core = g >> 1, g & 1
    ahead = (source // (2 * own) - chip) & 3
    slot = jnp.where(ahead == 2, 1, jnp.where(ahead == 1, 2, ahead))
    at = (((source // own) & 1) ^ core) * (4 * own) + slot * own + source % own
    spots = lax.broadcasted_iota(jnp.int32, (rows, rows), 0)
    mid_ref[...] = jnp.where(spots == at, 1.0, 0.0).T.astype(BF)
    for t in range(8):
        block = ((t + chip) & 3) * 2 + ((t // 4) ^ core)
        out_ref[t * own : (t + 1) * own] = mid_ref[pl.ds(pl.multiple_of(block * own, own), own)]


def sort_kernel(at, pick_ref, value_ref, *refs):
    kept_ref, out_ref = refs[-2:]
    half = kept_ref.shape[0]
    value = value_ref[...]
    high = value.astype(BF)
    low = (value - high.astype(F32)).astype(BF)
    pick = pick_ref[:, at : at + value.shape[0]]
    kept = jnp.dot(pick[:half], high, preferred_element_type=F32)
    kept += jnp.dot(pick[:half], low, preferred_element_type=F32)
    out = jnp.dot(pick[half:], high, preferred_element_type=F32)
    if len(refs) == 4:
        kept += refs[0][...]
        out += refs[1][...]
    kept_ref[...] = kept
    out_ref[...] = out.astype(out_ref.dtype)


def deal_kernel(kept_ref, got_ref, mine_ref, *out_refs):
    n = mine_ref.shape[0]
    mine_ref[...] = kept_ref[:n] + got_ref[:n].astype(F32)
    for i, out_ref in enumerate(out_refs):
        at = slice((i + 1) * n, (i + 2) * n)
        out_ref[...] = (kept_ref[at] + got_ref[at].astype(F32)).astype(BF)


def last_kernel(mine_ref, *refs):
    value = mine_ref[...]
    for ref in refs[:-1]:
        value += ref[...].astype(F32)
    refs[-1][...] = value.astype(BF)


def on_device(draft_rows, tree_sizes, draft_map, row_order, up_weight, down_weight):
    own, width = draft_rows.shape
    rows, hidden_units = row_order.shape[0], up_weight.shape[1]
    part = hidden_units // 4
    group = rows // 2
    chains = range(4)

    run = Line()
    fetched = [from_chip(draft_rows, ahead) for ahead in (2, 1, 3)]
    ups, draft = load(run, up_weight, draft_rows)
    column = pack(run, draft, *fetched)
    beside = other_core(column)

    project_flops = 2 * group * width * part

    def project(q, far, dtype):
        return run(
            functools.partial(up_kernel, q, far),
            pltpu.VMEM((group, part), dtype),
            column if q < 2 else beside,
            ups,
            flops=project_flops,
        )

    got = [swap(project(q, 1, BF), q) for q in chains]
    kept = [project(q, 0, F32) for q in chains]
    downs = load(run, down_weight.T)
    pick = run(
        index_kernel,
        pltpu.VMEM((rows, rows), BF),
        tree_sizes[None, :],
        draft_map[None, :],
        row_order[None, :],
        flops=rows * rows * 64,
        scratch=[pltpu.VMEM((rows, rows), BF)],
    )

    block = pltpu.VMEM((group // 2, part), BF)
    block32 = pltpu.VMEM((group // 2, part), F32)
    came = [swap(run(second_kernel, block, kept[q], got[q]), (q + 1) % 4) for q in chains]
    third = [run(third_kernel, [block32, block], kept[q], got[q], came[q]) for q in chains]
    came = [swap(third[q][1], (q + 2) % 4) for q in chains]
    fourth = [run(fourth_kernel, [block32, block], third[q][0], came[q]) for q in chains]
    came = [swap(fourth[q][1], (q + 3) % 4) for q in chains]
    erfs = group // 2 * part
    hidden = [run(gelu_kernel, block, fourth[q][0], came[q], erfs=erfs) for q in chains]

    whole = pltpu.VMEM((group, width), F32)

    def down_own(q, *after):
        return run(
            functools.partial(down_own_kernel, q),
            whole,
            hidden[q],
            more[q],
            hidden[q + 1],
            more[q + 1],
            downs,
            after=after,
            flops=2 * project_flops,
        )

    def down(q, total):
        return run(
            functools.partial(down_kernel, q),
            whole,
            total,
            near[q],
            far[q],
            downs,
            flops=project_flops,
        )

    def sort(at, total, dtype, *others):
        return run(
            functools.partial(sort_kernel, at),
            [whole, pltpu.VMEM((group, width), dtype)],
            pick,
            total,
            *others,
            flops=3 * group * group * width,
        )

    more = [swap(hidden[q], (q + 1) % 4) for q in chains]
    near, far = {}, {}
    for q, after in zip((1, 2, 3, 0), (hidden[3], more[0], more[1], more[2])):
        near[q] = swap(copied(run, hidden[q], after), q)
    far[1] = swap(copied(run, more[1], more[3]), 1)
    one = down_own(0)
    for q, after in zip((2, 3, 0), (near[1], near[2], near[3])):
        far[q] = swap(copied(run, more[q], after), q)
    two = down_own(2, near[0])
    one = down(1, one)
    two = down(3, down(2, two))
    others = sort(group, two, F32)
    kept, out = sort(0, down(0, one), BF, *others)
    row_block = pltpu.VMEM((own, width), BF)
    mine, one, two, three = run(
        deal_kernel,
        [pltpu.VMEM((own, width), F32), row_block, row_block, row_block],
        kept,
        other_core(out),
    )
    arrived = [from_chip(value, ahead) for ahead, value in ((2, two), (1, three), (3, one))]
    return run(last_kernel, jax.ShapeDtypeStruct((own, width), BF), mine, *arrived)


def solution(mesh):
    return jax.shard_map(
        on_device,
        mesh=mesh,
        in_specs=(
            P("gr", ("gc", "dr")),
            P(),
            P(),
            P(),
            P(("gc", "dr"), "gr"),
            P("gr", ("gc", "dr")),
        ),
        out_specs=P("gr", ("gc", "dr")),
        check_vma=False,
    )
```

```python
import functools

import jax
import jax.numpy as jnp
from jax import lax
from jax.experimental import pallas as pl
from jax.experimental.pallas import tpu as pltpu
from jax.sharding import PartitionSpec as P

BF, F32 = jnp.bfloat16, jnp.float32
YZ = ("gc", "dr")
LIMIT = 8 << 20


def place(y, z):
    return (y * 2 + z % 2) * 2 + z // 2


SIDES = ((1, 0, 3, 2), (3, 2, 1, 0))
SWAPS = tuple(
    [(place(y, z), place(side[y], z)) for y in range(4) for z in range(4)] for side in SIDES
) + tuple(
    [(place(y, z), place(y, side[z])) for y in range(4) for z in range(4)] for side in SIDES
)


def swap(value, side):
    return lax.ppermute(value, YZ, SWAPS[side])


def from_chip(value, ahead):
    pairs = [(((x + ahead) % 4) * 2 + c, x * 2 + c) for x in range(4) for c in range(2)]
    return lax.ppermute(value, "gr", pairs)


def other_core(value):
    return lax.ppermute(value, "gr", [(i, i ^ 1) for i in range(8)])


def square_bits(p):
    return (p & 1) ^ (p >> 1), p >> 1


class Line:
    def __init__(self):
        self.last = None

    def __call__(self, kernel, outs, *args, after=(), spaces=None, flops=0, moved=0, erfs=0, scratch=()):
        waits = [*after] if self.last is None else [self.last, *after]
        vmem = pl.BlockSpec(memory_space=pltpu.VMEM)
        specs = [vmem] * len(args) + [pl.BlockSpec(memory_space=pl.ANY)] * len(waits)
        for i, space in (spaces or {}).items():
            specs[i] = pl.BlockSpec(memory_space=space)
        single = not isinstance(outs, list)
        shapes = [outs] if single else outs
        moved = moved or sum(a.size * a.dtype.itemsize for a in args)

        def body(*refs):
            kernel(*refs[: len(args)], *refs[len(args) + len(waits) :])

        out = pl.pallas_call(
            body,
            out_shape=shapes,
            in_specs=specs,
            out_specs=[vmem] * len(shapes),
            scratch_shapes=list(scratch),
            compiler_params=pltpu.CompilerParams(vmem_limit_bytes=LIMIT),
            cost_estimate=pl.CostEstimate(flops=flops, bytes_accessed=moved, transcendentals=erfs),
        )(*args, *waits)
        self.last = out[0]
        return out[0] if single else out


def load_kernel(count, *refs):
    src, extras = refs[0], refs[1 : 1 + count]
    out, extra_outs, sems = refs[-2 - count], refs[-1 - count : -1], refs[-1]
    width = out.shape[2]
    copies = [
        pltpu.make_async_copy(src.at[:, pl.ds(i * width, width)], out.at[i], sems.at[i])
        for i in range(4)
    ]
    for i in range(count):
        copies.append(pltpu.make_async_copy(extras[i], extra_outs[i], sems.at[4 + i]))
    for copy in copies:
        copy.start()
    for copy in copies:
        copy.wait()


def load(run, weight, *extras):
    rows, columns = weight.shape
    count = len(extras)
    values = [pltpu.with_memory_space_constraint(v, pltpu.HBM) for v in (weight, *extras)]
    out = run(
        functools.partial(load_kernel, count),
        [pltpu.VMEM((4, rows, columns // 4), BF)] + [pltpu.VMEM(v.shape, v.dtype) for v in extras],
        *values,
        spaces={i: pltpu.HBM for i in range(1 + count)},
        moved=weight.size * 4,
        scratch=[pltpu.SemaphoreType.DMA((4 + count,))],
    )
    return out if extras else out[0]


def pack_kernel(*refs):
    out, at = refs[-1], 0
    for ref in refs[:-1]:
        out[at : at + ref.shape[0]] = ref[...]
        at += ref.shape[0]


def pack(run, *values):
    rows = sum(v.shape[0] for v in values)
    return run(pack_kernel, pltpu.VMEM((rows, values[0].shape[1]), BF), *values)


def copied(run, value, *after):
    return run(pack_kernel, pltpu.VMEM(value.shape, value.dtype), value, after=after)


def side_bit(side):
    gc = lax.axis_index("gc")
    if side % 4 < 2:
        return square_bits(gc >> 1)[side % 4]
    return square_bits(lax.axis_index("dr") * 2 + (gc & 1))[side % 4 - 2]


def quarter_of(q, far):
    return (q % 2) * 2 + (side_bit(q) ^ far)


def half_of(q, near, rows):
    return pl.ds(pl.multiple_of((side_bit(q + 1) ^ near) * rows, rows), rows)


def up_kernel(q, far, rows_ref, weight_ref, out_ref):
    half = out_ref.shape[0] // 2
    rows = jnp.concatenate([rows_ref[half_of(q, near, half)] for near in range(2)])
    quarter = quarter_of(q, far)
    width = weight_ref.shape[2]
    for start in range(0, width, 256):
        stop = min(start + 256, width)
        value = jnp.dot(rows, weight_ref[quarter, :, start:stop], preferred_element_type=F32)
        out_ref[:, start:stop] = value.astype(out_ref.dtype)


def second_kernel(kept_ref, got_ref, out_ref):
    n = out_ref.shape[0]
    out_ref[...] = (kept_ref[n:] + got_ref[n:].astype(F32)).astype(BF)


def third_kernel(kept_ref, got_ref, new_ref, sum_ref, out_ref):
    n = out_ref.shape[0]
    value = kept_ref[:n] + got_ref[:n].astype(F32) + new_ref[...].astype(F32)
    sum_ref[...] = value
    out_ref[...] = value.astype(BF)


def fourth_kernel(kept_ref, got_ref, sum_ref, out_ref):
    value = kept_ref[...] + got_ref[...].astype(F32)
    sum_ref[...] = value
    out_ref[...] = value.astype(BF)


def gelu_kernel(kept_ref, got_ref, out_ref):
    value = kept_ref[...] + got_ref[...].astype(F32)
    value = value * (1.0 + lax.erf(value * (2.0**-0.5))) * 0.5
    out_ref[...] = value.astype(BF)


def add_down(q, far, near_ref, far_ref, weight_ref, from_ref, out_ref):
    half = out_ref.shape[0] // 2
    value = lax.dot_general(
        jnp.concatenate([near_ref[...], far_ref[...]]),
        weight_ref[quarter_of(q, far)],
        (((1,), (1,)), ((), ())),
        preferred_element_type=F32,
    )
    for near in range(2):
        at = half_of(q, near, half)
        rows = value[near * half : (near + 1) * half]
        out_ref[at] = rows if from_ref is None else from_ref[at] + rows


def down_own_kernel(q, one, one_more, two, two_more, weight_ref, out_ref):
    add_down(q, 0, one, one_more, weight_ref, None, out_ref)
    add_down(q + 1, 0, two, two_more, weight_ref, out_ref, out_ref)


def down_kernel(q, total_ref, near_ref, far_ref, weight_ref, out_ref):
    add_down(q, 1, near_ref, far_ref, weight_ref, total_ref, out_ref)


def index_kernel(sizes_ref, map_ref, order_ref, out_ref, mid_ref):
    rows = order_ref.shape[1]
    reqs = sizes_ref.shape[1]
    own = rows // 8
    down_at = lax.broadcasted_iota(jnp.int32, (reqs, reqs), 0)
    along = lax.broadcasted_iota(jnp.int32, (reqs, reqs), 1)
    sizes, owner = sizes_ref[...], map_ref[...]

    def upright(row):
        return jnp.sum(jnp.where(down_at == along, row, 0), axis=1, keepdims=True)

    earlier = along < down_at
    owners = upright(owner)
    before = (owner < owners) | ((owner == owners) & earlier)
    start = jnp.sum(jnp.where(earlier, sizes, 0), axis=1, keepdims=True)
    shift = jnp.sum(jnp.where(before, sizes, 0), axis=1, keepdims=True) - start
    order = order_ref[...]
    inside = (order >= start) & (order < start + upright(sizes))
    source = order + jnp.sum(jnp.where(inside, shift, 0), axis=0, keepdims=True)
    g = lax.axis_index("gr")
    chip, core = g >> 1, g & 1
    ahead = (source // (2 * own) - chip) & 3
    slot = jnp.where(ahead == 2, 1, jnp.where(ahead == 1, 2, ahead))
    at = (((source // own) & 1) ^ core) * (4 * own) + slot * own + source % own
    spots = lax.broadcasted_iota(jnp.int32, (rows, rows), 0)
    mid_ref[...] = jnp.where(spots == at, 1.0, 0.0).T.astype(BF)
    for t in range(8):
        block = ((t + chip) & 3) * 2 + ((t // 4) ^ core)
        out_ref[t * own : (t + 1) * own] = mid_ref[pl.ds(pl.multiple_of(block * own, own), own)]


def sort_kernel(at, side, exact, pick_ref, value_ref, *refs):
    out_ref = refs[-1]
    half = out_ref.shape[0]
    value = value_ref[...]
    high = value.astype(BF)
    pick = pick_ref[side * half : (side + 1) * half, at : at + value.shape[0]]
    out = jnp.dot(pick, high, preferred_element_type=F32)
    if exact:
        low = (value - high.astype(F32)).astype(BF)
        out += jnp.dot(pick, low, preferred_element_type=F32)
    for ref in refs[:-1]:
        out += ref[...]
    out_ref[...] = out.astype(out_ref.dtype)


def deal_kernel(kept_ref, got_ref, mine_ref, *out_refs):
    n = mine_ref.shape[0]
    mine_ref[...] = kept_ref[:n] + got_ref[:n].astype(F32)
    for i, out_ref in enumerate(out_refs):
        at = slice((i + 1) * n, (i + 2) * n)
        out_ref[...] = (kept_ref[at] + got_ref[at].astype(F32)).astype(BF)


def last_kernel(mine_ref, *refs):
    value = mine_ref[...]
    for ref in refs[:-1]:
        value += ref[...].astype(F32)
    refs[-1][...] = value.astype(BF)


def on_device(draft_rows, tree_sizes, draft_map, row_order, up_weight, down_weight):
    own, width = draft_rows.shape
    rows, hidden_units = row_order.shape[0], up_weight.shape[1]
    part = hidden_units // 4
    group = rows // 2
    chains = range(4)

    run = Line()
    fetched = [from_chip(draft_rows, ahead) for ahead in (2, 1, 3)]
    ups, draft = load(run, up_weight, draft_rows)
    column = pack(run, draft, *fetched)
    beside = other_core(column)

    project_flops = 2 * group * width * part

    def project(q, far, dtype):
        return run(
            functools.partial(up_kernel, q, far),
            pltpu.VMEM((group, part), dtype),
            column if q < 2 else beside,
            ups,
            flops=project_flops,
        )

    got = [swap(project(q, 1, BF), q) for q in chains]
    kept = [project(q, 0, F32) for q in chains]
    downs = load(run, down_weight.T)
    pick = run(
        index_kernel,
        pltpu.VMEM((rows, rows), BF),
        tree_sizes[None, :],
        draft_map[None, :],
        row_order[None, :],
        flops=rows * rows * 64,
        scratch=[pltpu.VMEM((rows, rows), BF)],
    )

    block = pltpu.VMEM((group // 2, part), BF)
    block32 = pltpu.VMEM((group // 2, part), F32)
    came = [swap(run(second_kernel, block, kept[q], got[q]), (q + 1) % 4) for q in chains]
    third = [run(third_kernel, [block32, block], kept[q], got[q], came[q]) for q in chains]
    came = [swap(third[q][1], (q + 2) % 4) for q in chains]
    fourth = [run(fourth_kernel, [block32, block], third[q][0], came[q]) for q in chains]
    came = [swap(fourth[q][1], (q + 3) % 4) for q in chains]
    erfs = group // 2 * part
    hidden = [run(gelu_kernel, block, fourth[q][0], came[q], erfs=erfs) for q in chains]

    whole = pltpu.VMEM((group, width), F32)

    def down_own(q, *after):
        return run(
            functools.partial(down_own_kernel, q),
            whole,
            hidden[q],
            more[q],
            hidden[q + 1],
            more[q + 1],
            downs,
            after=after,
            flops=2 * project_flops,
        )

    def down(q, total):
        return run(
            functools.partial(down_kernel, q),
            whole,
            total,
            near[q],
            far[q],
            downs,
            flops=project_flops,
        )

    def sort(at, side, total, dtype, *others):
        return run(
            functools.partial(sort_kernel, at, side, side == 0),
            pltpu.VMEM((group, width), dtype),
            pick,
            total,
            *others,
            flops=2 * group * group * width,
        )

    more = [swap(hidden[q], (q + 1) % 4) for q in chains]
    near, far = {}, {}
    for q, after in zip((1, 2, 3, 0), (hidden[3], more[0], more[1], more[2])):
        near[q] = swap(copied(run, hidden[q], after), q)
    far[1] = swap(copied(run, more[1], more[3]), 1)
    one = down_own(0)
    for q, after in zip((2, 3, 0), (near[1], near[2], near[3])):
        far[q] = swap(copied(run, more[q], after), q)
    two = down_own(2, near[0])
    one = down(1, one)
    two = down(3, down(2, two))
    other = sort(group, 1, two, F32)
    one = down(0, one)
    out = other_core(sort(0, 1, one, BF, other))
    kept = sort(0, 0, one, F32, sort(group, 0, two, F32))
    row_block = pltpu.VMEM((own, width), BF)
    mine, one, two, three = run(
        deal_kernel,
        [pltpu.VMEM((own, width), F32), row_block, row_block, row_block],
        kept,
        out,
    )
    arrived = [from_chip(value, ahead) for ahead, value in ((2, two), (1, three), (3, one))]
    return run(last_kernel, jax.ShapeDtypeStruct((own, width), BF), mine, *arrived)


def solution(mesh):
    return jax.shard_map(
        on_device,
        mesh=mesh,
        in_specs=(
            P("gr", ("gc", "dr")),
            P(),
            P(),
            P(),
            P(("gc", "dr"), "gr"),
            P("gr", ("gc", "dr")),
        ),
        out_specs=P("gr", ("gc", "dr")),
        check_vma=False,
    )
```
